32 devices in a mesh: groups: 2 (over x), ctx: 16 (over z, y, core).
Axes of the slice: x: 2, y: 2, z: 4, core: 2. Of those that a mesh axis runs over, the one named last changes fastest.
Arguments:
- token_codes: int32 [4096, 3584], P(('groups', 'ctx')), parts along dimension 0, may hold values from 0 to 247, as said below
- scales: bfloat16 [4096], P(('groups', 'ctx')), parts along dimension 0, may hold values from 0.00390625 to 64
- routes: int32 [4096, 2], P(('groups', 'ctx')), parts along dimension 0, may hold values from 0 to 3, all different within a row; in each aligned block of 128 rows (0 to 127, 128 to 255, ...) at most 96 rows name the same one
- route_gates: float32 [4096, 2], P(('groups', 'ctx')), parts along dimension 0, may hold values from 0.1 to 1
- gate_proj: bfloat16 [16, 3584, 384], P('ctx'), may hold values from -0.09375 to 0.09375
- up_proj: bfloat16 [16, 3584, 384], P('ctx'), may hold values from -0.09375 to 0.09375
- down_proj: bfloat16 [16, 384, 3584], P('ctx'), may hold values from -0.15625 to 0.15625
Outputs:
- mixed: bfloat16 [4096, 3584], P(('groups', 'ctx')), parts along dimension 0
The draws below stay inside these ranges and needn't reach their ends.
There are 2 independent parts, one for each index of `groups`. The reference program is written for one: setup_inputs(seed, part) draws one part's arguments, and reference() takes and returns one part's arrays. A program takes and returns all parts, laid end to end along the dimension named above; an argument that names none is the same for every part. Nothing has to cross between parts.
Inputs may be any that keep to these rules, and one draw needn't show every extreme that they name: In each aligned block of 128 tokens (the tokens of one device) no expert is named by more than 96 routes, a bound that some block reaches; the 2 experts of a token differ. `token_codes`: no code has exponent field 15.
All inputs are finite; a program needn't handle non-finite values.
Results may differ from the reference program's by a relative error of at most 0.0057.
Values may be sent and summed in bfloat16 or wider, within the bound.
A program may use at most 128 MiB of HBM per device.

```python
import math
import jax
import jax.numpy as jnp
import numpy as np
from jax import lax

D = 3584
FF = 1536
SLICES = 4
TOP = 2
TOK_DEV = 128
FF_DEV = 384
EXPERTS = 4
CAP = 96
TOKENS = 2048
N_CTX = 16


def token_offsets(key):
    return jax.random.randint(jax.random.fold_in(key, 101), (TOKENS,), 0, 12)


def draw_token_codes(key, part):
    offsets = token_offsets(key)
    key = jax.random.fold_in(key, 7)
    sign_key, step_key, mantissa_key = jax.random.split(key, 3)
    shape = (TOKENS, D)
    sign_bit = jax.random.randint(sign_key, shape, 0, 2)
    steps_off = jax.random.randint(step_key, shape, -3, 4)
    exponent = jnp.maximum(offsets[:, None] + steps_off, 0)
    mantissa = jax.random.randint(mantissa_key, shape, 0, 8)
    return (sign_bit * 128 + exponent * 8 + mantissa).astype(jnp.int32)


def draw_scales(key, part):
    offsets = token_offsets(key)
    key = jax.random.fold_in(key, 11)
    factor = jnp.exp(jax.random.uniform(key, (TOKENS,), jnp.float32, math.log(0.5), math.log(2.0)))
    power = jnp.ones((TOKENS,), jnp.float32)
    for bit_no in range(4):
        step_factor = jnp.float32(2.0 ** 2 ** bit_no)
        power = power * jnp.where(offsets // 2 ** bit_no % 2 == 1, step_factor, jnp.float32(1.0))
    return (factor * jnp.float32(32.0) / power).astype(jnp.bfloat16)


def block_levels(rng, extent, pieces, least, largest):
    def one(dim, parts):
        draws = jax.random.uniform(jax.random.fold_in(jax.random.fold_in(rng, 6), dim), (parts,), jnp.float32, least / len(pieces), largest / len(pieces))
        return jnp.repeat(jnp.exp(draws), extent[dim] // parts).reshape((-1,) + (1,) * (len(extent) - dim - 1))

    factor_of = one(*pieces[0])
    for cut in pieces[1:]:
        factor_of = factor_of * one(*cut)
    return factor_of


def assign_block(rng, own, number, rows, number_of, top, bound, slope):
    sequence = jax.random.permutation(rng, number_of)
    heavy_load, common = load_shares(number_of, rows * top, bound, slope, True), load_shares(number_of, rows * top, bound, slope, False)
    places = jnp.arange(number_of)

    def named(sizes, offset_by):
        used = int((sizes > 0).sum())
        fixed = max(1, used // 4)
        moved = fixed + (places - fixed + offset_by * (used - fixed)) % max(1, number_of - fixed)
        return jnp.zeros((number_of,), jnp.int32).at[sequence[jnp.where(places < fixed, places, moved)]].set(jnp.asarray(sizes, jnp.int32))

    sizes = jnp.where(number % 4 == 0, named(heavy_load, number // 4), named(common, number - number // 4 - 1))
    mixed = jax.random.permutation(jax.random.fold_in(own, 3), number_of)
    giver, receiver = mixed[0:number_of // 2 * 2:2], mixed[1:number_of // 2 * 2:2]
    room = jnp.minimum(sizes[giver] - 1, bound - sizes[receiver]) // 2
    room = jnp.where((giver == sequence[0]) | (receiver == sequence[0]) | (sizes[receiver] == 0), 0, jnp.maximum(room, 0))
    moved = jax.random.randint(jax.random.fold_in(own, 4), (number_of // 2,), 0, 1 << 20) % (room + 1)
    sizes = sizes.at[giver].add(-moved).at[receiver].add(moved)
    labels = jnp.searchsorted(jnp.cumsum(sizes), jnp.arange(rows * top), side="right").astype(jnp.int32)
    listing = labels.reshape(top, rows).T
    listing = listing[jax.random.permutation(jax.random.fold_in(own, 1), rows)]
    offset_by = jax.random.randint(jax.random.fold_in(own, 2), (rows, 1), 0, top)
    return jnp.take_along_axis(listing, (jnp.arange(top)[None, :] + offset_by) % top, axis=1)


def load_shares(number_of, total, reach, slope, full):
    weights = [(1 << 20) // math.isqrt(standing ** slope) + 1 for standing in range(1, number_of + 1)]
    largest = reach if full else min(reach, max(-(-total // number_of), total * weights[0] // sum(weights)))
    least = 1 if total - largest >= number_of - 1 else 0
    counts, surplus = [largest] + [least] * (number_of - 1), total - largest - least * (number_of - 1)
    while surplus > 0:
        free = [i for i in range(1, number_of) if counts[i] < largest] or [i for i in range(1, number_of) if counts[i] < reach]
        whole, remaining = sum([weights[i] for i in free]), surplus
        for i in free:
            more = min(reach - counts[i], max(1, remaining * weights[i] // whole), surplus)
            counts[i] = counts[i] + more
            surplus = surplus - more
    return np.array(counts)


def centred(stream_key, extent, scale, most, shards=(), held_as=jnp.bfloat16):
    factor_of = block_levels(stream_key, extent, shards, -0.22, 0.18) if shards else 1.0
    entries = jax.random.normal(stream_key, extent, jnp.float32) * scale * factor_of
    return jnp.minimum(jnp.maximum(entries, -most), most).astype(held_as)


def setup_inputs(seed: int = 0, part: int = 0) -> dict:
    splits = jax.random.split(jax.random.key(seed), 8)
    own_keys = jax.random.split(jax.random.fold_in(splits[7], part), 8)
    token_codes = draw_token_codes(jax.random.fold_in(jax.random.fold_in(splits[7], part), 71), part)
    scales = draw_scales(jax.random.fold_in(jax.random.fold_in(splits[7], part), 71), part)
    routes_keys = jax.random.split(jax.random.fold_in(own_keys[2], 1), TOKENS // TOK_DEV)
    routes_turns = jax.random.permutation(jax.random.fold_in(own_keys[2], 3), TOKENS // TOK_DEV)
    routes = jax.vmap(lambda own, number: assign_block(jax.random.fold_in(own_keys[2], 2), own, number, TOK_DEV, EXPERTS, TOP, CAP, 2))(routes_keys, routes_turns).reshape((TOKENS, TOP))
    route_gates = jnp.clip(0.1 + 0.9 * jax.random.uniform(own_keys[3], (TOKENS, TOP), jnp.float32) ** block_levels(own_keys[3], (TOKENS, TOP), ((0, 16),), -0.2, 0.2), 0.1, 1.0)
    gate_proj = centred(splits[4], (EXPERTS * SLICES, D, FF_DEV), D ** -0.5, 0.09375, ((0, 16),))
    up_proj = centred(splits[5], (EXPERTS * SLICES, D, FF_DEV), D ** -0.5, 0.09375, ((0, 16),))
    down_proj = centred(splits[6], (EXPERTS * SLICES, FF_DEV, D), FF ** -0.5, 0.15625, ((0, 16),))
    return dict(token_codes=token_codes, scales=scales, routes=routes, route_gates=route_gates, gate_proj=gate_proj, up_proj=up_proj, down_proj=down_proj)


def decode(token_codes):
    sign_bit = token_codes // 128
    exponent = (token_codes // 8) % 16
    mantissa = (token_codes % 8).astype(jnp.float32)
    scaling = jnp.ones(token_codes.shape, jnp.float32)
    for bit_no in range(4):
        factor = jnp.float32(2.0 ** (2 ** bit_no))
        scaling = scaling * jnp.where((exponent // (2 ** bit_no)) % 2 == 1, factor, jnp.float32(1.0))
    normal = (8.0 + mantissa) * scaling * jnp.float32(2.0 ** -10)
    subnormal = mantissa * jnp.float32(2.0 ** -9)
    magnitude = jnp.where(exponent == 0, subnormal, normal)
    return jnp.where(sign_bit == 1, -magnitude, magnitude).astype(jnp.bfloat16)


def reference(token_codes, scales, routes, route_gates, gate_proj, up_proj, down_proj):
    values = decode(token_codes)
    route_total = TOKENS * TOP
    limit = N_CTX * CAP
    flat_ids = routes.reshape(-1)
    flat_gates = route_gates.reshape(-1)
    owner = jnp.arange(route_total, dtype=jnp.int32) // TOP

    def one_expert(accumulated, expert_no):
        routed = flat_ids == expert_no
        position = jnp.cumsum(routed.astype(jnp.int32)) - 1
        where_to = jnp.where(routed, position, limit).astype(jnp.int32)
        token_rows = jnp.zeros((limit,), jnp.int32).at[where_to].set(owner, mode="drop")
        weighting = jnp.zeros((limit,), jnp.float32).at[where_to].set(flat_gates, mode="drop")
        inputs = values[token_rows]
        row_scale = scales[token_rows].astype(jnp.float32)[:, None]
        start = (expert_no * SLICES).astype(jnp.int32)
        gate_block = lax.dynamic_slice_in_dim(gate_proj, start, SLICES, 0)
        up_block = lax.dynamic_slice_in_dim(up_proj, start, SLICES, 0)
        down_block = lax.dynamic_slice_in_dim(down_proj, start, SLICES, 0)
        result = jnp.zeros((limit, D), jnp.float32)
        for member_no in range(SLICES):
            gate_act = jnp.dot(inputs, gate_block[member_no], preferred_element_type=jnp.float32) * row_scale
            up_act = jnp.dot(inputs, up_block[member_no], preferred_element_type=jnp.float32) * row_scale
            hidden = (jax.nn.silu(gate_act) * up_act).astype(jnp.bfloat16)
            partial_value = jnp.dot(hidden, down_block[member_no], preferred_element_type=jnp.float32).astype(jnp.bfloat16)
            partial_value = lax.optimization_barrier(partial_value)
            result = result + partial_value.astype(jnp.float32)
        accumulated = accumulated.at[token_rows].add(weighting[:, None] * result)
        return accumulated, None

    mixed, _ = lax.scan(one_expert, jnp.zeros((TOKENS, D), jnp.float32), jnp.arange(EXPERTS, dtype=jnp.int32))
    return mixed.astype(jnp.bfloat16)
```

```python
import functools

import jax
import jax.numpy as jnp
from jax import lax
from jax.experimental import pallas as pl
from jax.experimental.pallas import tpu as pltpu
from jax.sharding import PartitionSpec as P

SLICES = 4
LANES = 128
BF16 = jnp.bfloat16
F32 = jnp.float32


def decode(codes):
    exponent = (codes >> 3) & 15
    mantissa = codes & 7
    whole = jnp.where(exponent > 0, (mantissa + 8) << exponent, mantissa << 1)
    whole = jnp.where(codes >= 128, -whole, whole)
    return (whole.astype(F32) * F32(2.0**-10)).astype(BF16)


def kernel(
    experts, slot, tile,
    codes, scales, routes, gates, gate_hbm, up_hbm, down_hbm,
    out,
    w_gu, w_down, pack, recv, gu, hid, part, krecv, ysend, yrecv, hsend, hrecv,
    w_sem, z_s, z_r, y_s, y_r, c_s, c_r, l_s, l_r, k_s, k_r, q_s, q_r, h_s, h_r,
):
    tok, width = codes.shape
    ff = down_hbm.shape[1]
    quarter = SLICES * slot
    total = experts * slot
    group = lax.axis_index("groups")
    me = lax.axis_index("ctx")
    z, row, core = me // 4, (me // 2) % 2, me % 2

    def device(zz, yy, cc):
        return (group, zz * 4 + yy * 2 + cc)

    def ahead(step):
        return (z + step) % experts

    def behind(step):
        return (z + experts - step) % experts

    def remote(src, dst, send, arrive, to):
        return pltpu.make_async_remote_copy(
            src_ref=src, dst_ref=dst, send_sem=send, recv_sem=arrive,
            device_id=to, device_id_type=pl.DeviceIdType.MESH,
        )

    other_core = device(z, row, 1 - core)
    other_row = device(z, 1 - row, core)

    barrier = pltpu.get_barrier_semaphore()
    pl.semaphore_signal(barrier, inc=1, device_id=other_core, device_id_type=pl.DeviceIdType.MESH)
    pl.semaphore_signal(barrier, inc=1, device_id=other_row, device_id_type=pl.DeviceIdType.MESH)
    for step in range(1, experts):
        pl.semaphore_signal(
            barrier, inc=1, device_id=device(ahead(step), row, core),
            device_id_type=pl.DeviceIdType.MESH,
        )

    loads = [
        pltpu.make_async_copy(gate_hbm.at[0], w_gu.at[:, pl.ds(0, ff)], w_sem.at[0]),
        pltpu.make_async_copy(up_hbm.at[0], w_gu.at[:, pl.ds(ff, ff)], w_sem.at[1]),
        pltpu.make_async_copy(down_hbm.at[0], w_down, w_sem.at[2]),
    ]
    for load in loads:
        load.start()

    lane = lax.broadcasted_iota(jnp.int32, (tok, LANES), 1)
    named = []
    for k in range(2):
        rel = routes[:, k : k + 1] - z
        rel = jnp.where(rel < 0, rel + experts, rel)
        named.append(rel)
    hits = [(lane == rel).astype(F32) for rel in named]
    lower = (
        lax.broadcasted_iota(jnp.int32, (tok, tok), 0)
        > lax.broadcasted_iota(jnp.int32, (tok, tok), 1)
    ).astype(F32).astype(BF16)
    ranks = jnp.dot(lower, (hits[0] + hits[1]).astype(BF16), preferred_element_type=F32)
    places = lax.broadcasted_iota(jnp.int32, (tok, total), 1).astype(F32)
    chosen = []
    for k in range(2):
        rank = jnp.sum(ranks * hits[k], axis=1, keepdims=True)
        place = named[k].astype(F32) * F32(slot) + rank
        chosen.append((places == place).astype(F32))
    chooser = (chosen[0] + chosen[1]).T.astype(BF16)
    mixing = gates[:, 0:1] * chosen[0] + gates[:, 1:2] * chosen[1]
    mix_hi = mixing.astype(BF16)
    mix_lo = (mixing - mix_hi.astype(F32)).astype(BF16)

    own = pl.multiple_of((row * 2 + core) * slot, 16)
    packed_scale = jnp.dot(chooser, scales[...], preferred_element_type=F32).astype(BF16)
    recv[pl.ds(own, slot), pl.ds(width, LANES)] = packed_scale[:slot]
    pack[:, pl.ds(width, LANES)] = packed_scale[slot:]

    @pl.loop(0, width // tile)
    def _(n):
        cols = pl.ds(pl.multiple_of(n * tile, tile), tile)
        rows = jnp.dot(chooser, decode(codes[:, cols]), preferred_element_type=F32).astype(BF16)
        recv[pl.ds(own, slot), cols] = rows[:slot]
        pack[:, cols] = rows[slot:]

    pl.semaphore_wait(barrier, experts + 1)

    def packet(step, yy, cc):
        return recv.at[pl.ds(pl.multiple_of(step * quarter + (yy * 2 + cc) * slot, 16), slot)]

    def slab(ref, step):
        return ref.at[pl.ds(pl.multiple_of(step * slot, 16), slot)]

    def send_z(step):
        return remote(
            slab(pack, step - 1), packet(step, row, core), z_s.at[step], z_r.at[step],
            device(ahead(step), row, core),
        )

    def send_y(step):
        src = packet(step, row, core)
        return remote(src, src, y_s.at[step], y_r.at[step], other_row)

    def send_c(step):
        src = packet(step, row, core)
        return remote(src, src, c_s.at[step], c_r.at[step], other_core)

    def send_l(step):
        src = packet(step, 1 - row, core)
        return remote(src, src, l_s.at[step], l_r.at[step], other_core)

    def part_rows(step, yy, cc):
        start = (step % 2) * quarter + (yy * 2 + cc) * slot
        return pl.ds(pl.multiple_of(start, 16), slot)

    def kept(step, yy):
        return pl.ds(pl.multiple_of((step * 2 + yy) * slot, 16), slot)

    def send_k(step, yy):
        return remote(
            part.at[part_rows(step, yy, 1 - core)], krecv.at[kept(step, yy)],
            k_s.at[step * 2 + yy], k_r.at[step * 2 + yy], other_core,
        )

    def send_q(step):
        return remote(
            slab(ysend, step % 2), slab(yrecv, step), q_s.at[step], q_r.at[step], other_row
        )

    def send_h(step):
        return remote(
            slab(hsend, step), slab(hrecv, step), h_s.at[step], h_r.at[step],
            device(behind(step), row, core),
        )

    for step in range(1, experts):
        send_z(step).start()
    send_y(0).start()
    send_c(0).start()
    for load in loads:
        load.wait()

    def finish(step):
        send_k(step, row).wait_recv()
        send_q(step).wait_recv()

        @pl.loop(0, width // tile)
        def _(n):
            cols = pl.ds(pl.multiple_of(n * tile, tile), tile)
            value = (
                part[part_rows(step, row, core), cols].astype(F32)
                + krecv[kept(step, row), cols].astype(F32)
                + slab(yrecv, step)[:, cols].astype(F32)
            ).astype(BF16)

            @pl.when(step > 0)
            def _():
                hsend[pl.ds(pl.multiple_of(step * slot, 16), slot), cols] = value

            @pl.when(step == 0)
            def _():
                hrecv[pl.ds(0, slot), cols] = value

        @pl.when(step > 0)
        def _():
            send_h(step).start()

        send_k(step, 0).wait_send()
        send_k(step, 1).wait_send()

    def one_group(step, carry):
        @pl.when(step + 1 < experts)
        def _():
            send_z(step + 1).wait_recv()
            send_y(step + 1).start()
            send_c(step + 1).start()

        send_y(step).wait_recv()
        send_l(step).start()
        send_c(step).wait_recv()
        send_l(step).wait_recv()

        rows = pl.ds(pl.multiple_of(step * quarter, 16), quarter)

        @pl.loop(0, 2 * ff // 256)
        def _(n):
            cols = pl.ds(pl.multiple_of(n * 256, 256), 256)
            gu[:, cols] = jnp.dot(
                recv[rows, pl.ds(0, width)], w_gu[:, cols], preferred_element_type=F32
            )

        @pl.loop(0, SLICES)
        def _(n):
            some = pl.ds(pl.multiple_of(n * slot, 16), slot)
            where = pl.ds(pl.multiple_of(step * quarter + n * slot, 16), slot)
            scale = recv[where, pl.ds(width, LANES)].astype(F32)[:, :1]
            a = gu[some, pl.ds(0, ff)] * scale
            b = gu[some, pl.ds(ff, ff)] * scale
            hid[some, :] = (a / (1.0 + jnp.exp(-a)) * b).astype(BF16)

        base = pl.ds(pl.multiple_of((step % 2) * quarter, 16), quarter)

        @pl.loop(0, width // tile)
        def _(n):
            cols = pl.ds(pl.multiple_of(n * tile, tile), tile)
            part[base, cols] = jnp.dot(
                hid[...], w_down[:, cols], preferred_element_type=F32
            ).astype(BF16)

        send_k(step, 1 - row).start()
        send_k(step, row).start()

        @pl.when(step >= 2)
        def _():
            send_q(step - 2).wait_send()

        send_k(step, 1 - row).wait_recv()

        @pl.loop(0, width // tile)
        def _(n):
            cols = pl.ds(pl.multiple_of(n * tile, tile), tile)
            ysend[pl.ds(pl.multiple_of((step % 2) * slot, 16), slot), cols] = (
                part[part_rows(step, 1 - row, core), cols].astype(F32)
                + krecv[kept(step, 1 - row), cols].astype(F32)
            ).astype(BF16)

        send_q(step).start()

        @pl.when(step > 0)
        def _():
            finish(step - 1)

        return carry

    lax.fori_loop(0, experts, one_group, 0)
    finish(experts - 1)

    for step in range(1, experts):
        send_h(step).wait_recv()

    @pl.loop(0, width // tile)
    def _(n):
        cols = pl.ds(pl.multiple_of(n * tile, tile), tile)
        rows = hrecv[:, cols]
        out[:, cols] = (
            jnp.dot(mix_hi, rows, preferred_element_type=F32)
            + jnp.dot(mix_lo, rows, preferred_element_type=F32)
        ).astype(BF16)

    for step in range(experts):
        send_y(step).wait_send()
        send_c(step).wait_send()
        send_l(step).wait_send()
        if step >= experts - 2:
            send_q(step).wait_send()
        if step > 0:
            send_z(step).wait_send()
            send_h(step).wait_send()


def local(token_codes, scales, routes, route_gates, gate_proj, up_proj, down_proj):
    tok, width = token_codes.shape
    ff = gate_proj.shape[2]
    experts = lax.axis_size("ctx") // SLICES
    cap = 3 * tok * routes.shape[1] // (2 * experts)
    slot = -(-cap // 16) * 16
    total = experts * slot
    vmem = pl.BlockSpec(memory_space=pltpu.VMEM)
    hbm = pl.BlockSpec(memory_space=pl.ANY)
    dma = pltpu.SemaphoreType.DMA
    return pl.pallas_call(
        functools.partial(kernel, experts, slot, 512),
        out_shape=jax.ShapeDtypeStruct((tok, width), BF16),
        in_specs=[vmem] * 4 + [hbm] * 3,
        out_specs=vmem,
        scratch_shapes=[
            pltpu.VMEM((width, 2 * ff), BF16),
            pltpu.VMEM((ff, width), BF16),
            pltpu.VMEM((total - slot, width + LANES), BF16),
            pltpu.VMEM((SLICES * total, width + LANES), BF16),
            pltpu.VMEM((SLICES * slot, 2 * ff), F32),
            pltpu.VMEM((SLICES * slot, ff), BF16),
            pltpu.VMEM((2 * SLICES * slot, width), BF16),
            pltpu.VMEM((2 * total, width), BF16),
            pltpu.VMEM((2 * slot, width), BF16),
            pltpu.VMEM((total, width), BF16),
            pltpu.VMEM((total, width), BF16),
            pltpu.VMEM((total, width), BF16),
            dma((3,)),
            dma((experts,)), dma((experts,)), dma((experts,)), dma((experts,)),
            dma((experts,)), dma((experts,)), dma((experts,)), dma((experts,)),
            dma((2 * experts,)), dma((2 * experts,)),
            dma((experts,)), dma((experts,)), dma((experts,)), dma((experts,)),
        ],
        compiler_params=pltpu.CompilerParams(
            collective_id=0, has_side_effects=True, vmem_limit_bytes=60 * 2**20
        ),
    )(
        token_codes,
        jnp.broadcast_to(scales[:, None], (tok, LANES)),
        routes,
        route_gates,
        gate_proj,
        up_proj,
        down_proj,
    )


def solution(mesh):
    placed = (
        P(("groups", "ctx"), None),
        P(("groups", "ctx")),
        P(("groups", "ctx"), None),
        P(("groups", "ctx"), None),
        P("ctx", None, None),
        P("ctx", None, None),
        P("ctx", None, None),
    )
    return jax.shard_map(
        local, mesh=mesh, in_specs=placed, out_specs=P(("groups", "ctx"), None), check_vma=False
    )
```

```python
import functools

import jax
import jax.numpy as jnp
from jax import lax
from jax.experimental import pallas as pl
from jax.experimental.pallas import tpu as pltpu
from jax.sharding import PartitionSpec as P

SLICES = 4
LANES = 128
CHUNKS = 4
BF16 = jnp.bfloat16
F32 = jnp.float32


def decode(codes):
    exponent = (codes >> 3) & 15
    mantissa = codes & 7
    whole = jnp.where(exponent > 0, (mantissa + 8) << exponent, mantissa << 1)
    whole = jnp.where(codes >= 128, -whole, whole)
    return (whole.astype(F32) * F32(2.0**-10)).astype(BF16)


def kernel(
    experts, slot, tile,
    codes, scales, routes, gates, gate_hbm, up_hbm, down_hbm,
    out,
    w_gu, w_down, pack, recv, gu, hid, mine, hsend, hrecv,
    w_sem, z_s, z_r, y_s, y_r, c_s, c_r, l_s, l_r, v_s, v_r, h_s, h_r,
    wy_s, wy_r, wx_s, wx_r, wl_s, wl_r, wm_s, wm_r, wc_s, wc_r,
):
    tok, width = codes.shape
    ff = down_hbm.shape[1]
    quarter = SLICES * slot
    total = experts * slot
    group = lax.axis_index("groups")
    groups = lax.axis_size("groups")
    me = lax.axis_index("ctx")
    z, row, core = me // 4, (me // 2) % 2, me % 2

    def device(zz, yy, cc):
        return (group, zz * 4 + yy * 2 + cc)

    def ahead(step):
        return (z + step) % experts

    def behind(step):
        return (z + experts - step) % experts

    def remote(src, dst, send, arrive, to):
        return pltpu.make_async_remote_copy(
            src_ref=src, dst_ref=dst, send_sem=send, recv_sem=arrive,
            device_id=to, device_id_type=pl.DeviceIdType.MESH,
        )

    other_core = device(z, row, 1 - core)
    other_row = device(z, 1 - row, core)

    other_both = device(z, 1 - row, 1 - core)
    block, far_block = row * 2 + core, (1 - row) * 2 + core

    def replica(ahead_by):
        return ((group + ahead_by) % groups, me)

    barrier = pltpu.get_barrier_semaphore()
    partners = [other_core, other_row, other_both]
    partners += [device(ahead(step), row, core) for step in range(1, experts)]
    partners += [replica(by) for by in range(1, groups)]
    for partner in partners:
        pl.semaphore_signal(
            barrier, inc=1, device_id=partner, device_id_type=pl.DeviceIdType.MESH
        )

    def block_rows(which):
        return pl.ds(pl.multiple_of(which * ff, 16), ff)

    loads = [
        pltpu.make_async_copy(gate_hbm.at[0], w_gu.at[:, pl.ds(0, ff)], w_sem.at[0]),
        pltpu.make_async_copy(up_hbm.at[0], w_gu.at[:, pl.ds(ff, ff)], w_sem.at[1]),
        pltpu.make_async_copy(down_hbm.at[0], w_down.at[block_rows(block)], w_sem.at[2]),
    ]
    for load in loads:
        load.start()
    pl.semaphore_wait(barrier, len(partners))

    share = ff // groups
    piece = width // CHUNKS

    def share_rows(which, owner):
        return pl.ds(pl.multiple_of(which * ff + owner * share, 16), share)

    def down_y(q):
        return remote(
            down_hbm.at[0, pl.ds(pl.multiple_of(group * share, 16), share), pl.ds(q * piece, piece)],
            w_down.at[share_rows(block, group), pl.ds(q * piece, piece)],
            wy_s.at[q], wy_r.at[q], other_row,
        )

    def down_x(by, q):
        src = w_down.at[share_rows(far_block, group), pl.ds(q * piece, piece)]
        at = (by - 1) * CHUNKS + q
        return remote(src, src, wx_s.at[at], wx_r.at[at], replica(by))

    def down_l(q):
        src = w_down.at[share_rows(far_block, group), pl.ds(q * piece, piece)]
        return remote(src, src, wl_s.at[q], wl_r.at[q], other_core)

    def down_m(by):
        src = w_down.at[share_rows(far_block, (group + groups - by) % groups)]
        return remote(src, src, wm_s.at[by - 1], wm_r.at[by - 1], other_core)

    down_c = remote(
        down_hbm.at[0], w_down.at[block_rows(block)], wc_s.at[0], wc_r.at[0], other_core
    )

    def relay(q):
        down_y(q).wait_recv()
        for by in range(1, groups):
            down_x(by, q).start()
        down_l(q).start()
        if q + 2 < CHUNKS:
            down_y(q + 2).start()

    down_y(0).start()
    down_y(1).start()
    down_c.start()

    lane = lax.broadcasted_iota(jnp.int32, (tok, LANES), 1)
    named = []
    for k in range(2):
        rel = routes[:, k : k + 1] - z
        rel = jnp.where(rel < 0, rel + experts, rel)
        named.append(rel)
    hits = [(lane == rel).astype(F32) for rel in named]
    lower = (
        lax.broadcasted_iota(jnp.int32, (tok, tok), 0)
        > lax.broadcasted_iota(jnp.int32, (tok, tok), 1)
    ).astype(F32).astype(BF16)
    ranks = jnp.dot(lower, (hits[0] + hits[1]).astype(BF16), preferred_element_type=F32)
    places = lax.broadcasted_iota(jnp.int32, (tok, total), 1).astype(F32)
    chosen = []
    for k in range(2):
        rank = jnp.sum(ranks * hits[k], axis=1, keepdims=True)
        place = named[k].astype(F32) * F32(slot) + rank
        chosen.append((places == place).astype(F32))
    chooser = (chosen[0] + chosen[1]).T.astype(BF16)
    mixing = gates[:, 0:1] * chosen[0] + gates[:, 1:2] * chosen[1]
    mix_hi = mixing.astype(BF16)
    mix_lo = (mixing - mix_hi.astype(F32)).astype(BF16)

    own = pl.multiple_of((row * 2 + core) * slot, 16)
    packed_scale = jnp.dot(chooser, scales[...], preferred_element_type=F32).astype(BF16)
    recv[pl.ds(own, slot), pl.ds(width, LANES)] = packed_scale[:slot]
    pack[:, pl.ds(width, LANES)] = packed_scale[slot:]

    @pl.loop(0, width // tile)
    def _(n):
        cols = pl.ds(pl.multiple_of(n * tile, tile), tile)
        rows = jnp.dot(chooser, decode(codes[:, cols]), preferred_element_type=F32).astype(BF16)
        recv[pl.ds(own, slot), cols] = rows[:slot]
        pack[:, cols] = rows[slot:]

    def packet(step, yy, cc):
        return recv.at[pl.ds(pl.multiple_of(step * quarter + (yy * 2 + cc) * slot, 16), slot)]

    def slab(ref, step):
        return ref.at[pl.ds(pl.multiple_of(step * slot, 16), slot)]

    def send_z(step):
        return remote(
            slab(pack, step - 1), packet(step, row, core), z_s.at[step], z_r.at[step],
            device(ahead(step), row, core),
        )

    def send_y(step):
        src = packet(step, row, core)
        return remote(src, src, y_s.at[step], y_r.at[step], other_row)

    def send_c(step):
        src = packet(step, row, core)
        return remote(src, src, c_s.at[step], c_r.at[step], other_core)

    def send_l(step):
        src = packet(step, 1 - row, core)
        return remote(src, src, l_s.at[step], l_r.at[step], other_core)

    def hid_rows(step, yy, cc):
        return pl.ds(pl.multiple_of(step * quarter + (yy * 2 + cc) * slot, 16), slot)

    def step_rows(step):
        return pl.ds(pl.multiple_of(step * slot, 16), slot)

    own_cols = pl.ds(pl.multiple_of(block * ff, LANES), ff)

    def send_v(step, number):
        yy = 1 - row if number > 0 else row
        cc = 1 - core if number != 1 else core
        return remote(
            hid.at[hid_rows(step, yy, cc)], mine.at[step_rows(step), own_cols],
            v_s.at[step * 3 + number], v_r.at[step * 3 + number], device(z, yy, cc),
        )

    def send_h(step):
        return remote(
            slab(hsend, step), slab(hrecv, step), h_s.at[step], h_r.at[step],
            device(behind(step), row, core),
        )

    def spread(step):
        send_y(step).start()
        send_c(step).start()

    def hidden(step):
        send_y(step).wait_recv()
        send_l(step).start()
        send_c(step).wait_recv()
        send_l(step).wait_recv()
        rows = pl.ds(pl.multiple_of(step * quarter, 16), quarter)

        @pl.loop(0, 2 * ff // 256)
        def _(n):
            cols = pl.ds(pl.multiple_of(n * 256, 256), 256)
            gu[:, cols] = jnp.dot(
                recv[rows, pl.ds(0, width)], w_gu[:, cols], preferred_element_type=F32
            )

        @pl.loop(0, SLICES)
        def _(n):
            some = pl.ds(pl.multiple_of(n * slot, 16), slot)
            where = pl.ds(pl.multiple_of(step * quarter + n * slot, 16), slot)
            scale = recv[where, pl.ds(width, LANES)].astype(F32)[:, :1]
            a = gu[some, pl.ds(0, ff)] * scale
            b = gu[some, pl.ds(ff, ff)] * scale
            hid[where, :] = (a / (1.0 + jnp.exp(-a)) * b).astype(BF16)

        for number in range(3):
            send_v(step, number).start()
        mine[step_rows(step), own_cols] = hid[hid_rows(step, row, core), :]

    def project(step, target):
        for number in range(3):
            send_v(step, number).wait_recv()

        @pl.loop(0, width // tile)
        def _(n):
            cols = pl.ds(pl.multiple_of(n * tile, tile), tile)
            target[step_rows(step), cols] = jnp.dot(
                mine[step_rows(step), :], w_down[:, cols], preferred_element_type=F32
            ).astype(BF16)

    send_z(1).start()
    relay(0)
    relay(1)
    send_z(1).wait_recv()
    spread(1)
    if experts > 2:
        send_z(2).start()
    for q in range(2, CHUNKS):
        relay(q)
    for load in loads:
        load.wait()
    hidden(1)
    for by in range(1, groups):
        for q in range(CHUNKS):
            down_x(by, q).wait_recv()
        down_m(by).start()

    def one_group(step, carry):
        @pl.when(step + 1 < experts)
        def _():
            send_z(step + 1).wait_recv()
            spread(step + 1)

        @pl.when(step + 2 < experts)
        def _():
            send_z(step + 2).start()

        @pl.when(step == 1)
        def _():
            down_c.wait_recv()
            for q in range(CHUNKS):
                down_l(q).wait_recv()
            for by in range(1, groups):
                down_m(by).wait_recv()

        project(step, hsend)
        send_h(step).start()

        @pl.when(step == experts - 2)
        def _():
            spread(0)

        @pl.when(step + 1 < experts)
        def _():
            hidden(step + 1)

        return carry

    lax.fori_loop(1, experts, one_group, 0)
    hidden(0)
    project(0, hrecv)

    for step in range(1, experts):
        send_h(step).wait_recv()

    @pl.loop(0, width // tile)
    def _(n):
        cols = pl.ds(pl.multiple_of(n * tile, tile), tile)
        rows = hrecv[:, cols]
        out[:, cols] = (
            jnp.dot(mix_hi, rows, preferred_element_type=F32)
            + jnp.dot(mix_lo, rows, preferred_element_type=F32)
        ).astype(BF16)

    for q in range(CHUNKS):
        down_y(q).wait_send()
        down_l(q).wait_send()
        for by in range(1, groups):
            down_x(by, q).wait_send()
    for by in range(1, groups):
        down_m(by).wait_send()
    down_c.wait_send()
    for step in range(experts):
        send_y(step).wait_send()
        send_c(step).wait_send()
        send_l(step).wait_send()
        for number in range(3):
            send_v(step, number).wait_send()
        if step > 0:
            send_z(step).wait_send()
            send_h(step).wait_send()


def local(token_codes, scales, routes, route_gates, gate_proj, up_proj, down_proj):
    tok, width = token_codes.shape
    ff = gate_proj.shape[2]
    experts = lax.axis_size("ctx") // SLICES
    cap = 3 * tok * routes.shape[1] // (2 * experts)
    slot = -(-cap // 16) * 16
    total = experts * slot
    vmem = pl.BlockSpec(memory_space=pltpu.VMEM)
    hbm = pl.BlockSpec(memory_space=pl.ANY)
    dma = pltpu.SemaphoreType.DMA
    groups = lax.axis_size("groups")
    far = max(1, (groups - 1) * CHUNKS)
    return pl.pallas_call(
        functools.partial(kernel, experts, slot, 512),
        out_shape=jax.ShapeDtypeStruct((tok, width), BF16),
        in_specs=[vmem] * 4 + [hbm] * 3,
        out_specs=vmem,
        scratch_shapes=[
            pltpu.VMEM((width, 2 * ff), BF16),
            pltpu.VMEM((SLICES * ff, width), BF16),
            pltpu.VMEM((total - slot, width + LANES), BF16),
            pltpu.VMEM((SLICES * total, width + LANES), BF16),
            pltpu.VMEM((SLICES * slot, 2 * ff), F32),
            pltpu.VMEM((SLICES * total, ff), BF16),
            pltpu.VMEM((total, SLICES * ff), BF16),
            pltpu.VMEM((total, width), BF16),
            pltpu.VMEM((total, width), BF16),
            dma((3,)),
            dma((experts,)), dma((experts,)), dma((experts,)), dma((experts,)),
            dma((experts,)), dma((experts,)), dma((experts,)), dma((experts,)),
            dma((3 * experts,)), dma((3 * experts,)),
            dma((experts,)), dma((experts,)),
            dma((CHUNKS,)), dma((CHUNKS,)), dma((far,)), dma((far,)),
            dma((CHUNKS,)), dma((CHUNKS,)), dma((groups,)), dma((groups,)),
            dma((1,)), dma((1,)),
        ],
        compiler_params=pltpu.CompilerParams(
            collective_id=0, has_side_effects=True, vmem_limit_bytes=60 * 2**20
        ),
    )(
        token_codes,
        jnp.broadcast_to(scales[:, None], (tok, LANES)),
        routes,
        route_gates,
        gate_proj,
        up_proj,
        down_proj,
    )


def solution(mesh):
    placed = (
        P(("groups", "ctx"), None),
        P(("groups", "ctx")),
        P(("groups", "ctx"), None),
        P(("groups", "ctx"), None),
        P("ctx", None, None),
        P("ctx", None, None),
        P("ctx", None, None),
    )
    return jax.shard_map(
        local, mesh=mesh, in_specs=placed, out_specs=P(("groups", "ctx"), None), check_vma=False
    )
```

```python
import functools

import jax
import jax.numpy as jnp
from jax import lax
from jax.experimental import pallas as pl
from jax.experimental.pallas import tpu as pltpu
from jax.sharding import PartitionSpec as P

SLICES = 4
LANES = 128
CHUNKS = 4
BF16 = jnp.bfloat16
F32 = jnp.float32


def decode(codes):
    exponent = (codes >> 3) & 15
    mantissa = codes & 7
    whole = jnp.where(exponent > 0, (mantissa + 8) << exponent, mantissa << 1)
    whole = jnp.where(codes >= 128, -whole, whole)
    return (whole.astype(F32) * F32(2.0**-10)).astype(BF16)


def kernel(
    experts, slot, tile,
    codes, scales, routes, gates, gate_hbm, up_hbm, down_hbm,
    out,
    w_gu, w_down, pack, recv, gu, hid, mine, hsend, hrecv,
    w_sem, z_s, z_r, y_s, y_r, c_s, c_r, l_s, l_r, v_s, v_r, h_s, h_r,
    wy_s, wy_r, wx_s, wx_r, wl_s, wl_r, wm_s, wm_r, wc_s, wc_r,
):
    tok, width = codes.shape
    ff = down_hbm.shape[1]
    quarter = SLICES * slot
    total = experts * slot
    group = lax.axis_index("groups")
    groups = lax.axis_size("groups")
    me = lax.axis_index("ctx")
    z, row, core = me // 4, (me // 2) % 2, me % 2

    def device(zz, yy, cc):
        return (group, zz * 4 + yy * 2 + cc)

    def ahead(step):
        return (z + step) % experts

    def behind(step):
        return (z + experts - step) % experts

    def remote(src, dst, send, arrive, to):
        return pltpu.make_async_remote_copy(
            src_ref=src, dst_ref=dst, send_sem=send, recv_sem=arrive,
            device_id=to, device_id_type=pl.DeviceIdType.MESH,
        )

    other_core = device(z, row, 1 - core)
    other_row = device(z, 1 - row, core)

    other_both = device(z, 1 - row, 1 - core)
    block, far_block = row * 2 + core, (1 - row) * 2 + core

    def replica(ahead_by):
        return ((group + ahead_by) % groups, me)

    barrier = pltpu.get_barrier_semaphore()
    partners = [other_core, other_row, other_both]
    partners += [device(ahead(step), row, core) for step in range(1, experts)]
    partners += [replica(by) for by in range(1, groups)]
    for partner in partners:
        pl.semaphore_signal(
            barrier, inc=1, device_id=partner, device_id_type=pl.DeviceIdType.MESH
        )

    def block_rows(which):
        return pl.ds(pl.multiple_of(which * ff, 16), ff)

    loads = [
        pltpu.make_async_copy(gate_hbm.at[0], w_gu.at[:, pl.ds(0, ff)], w_sem.at[0]),
        pltpu.make_async_copy(up_hbm.at[0], w_gu.at[:, pl.ds(ff, ff)], w_sem.at[1]),
        pltpu.make_async_copy(down_hbm.at[0], w_down.at[block_rows(block)], w_sem.at[2]),
    ]
    for load in loads:
        load.start()
    pl.semaphore_wait(barrier, len(partners))

    share = ff // groups
    piece = width // CHUNKS

    def share_rows(which, owner):
        return pl.ds(pl.multiple_of(which * ff + owner * share, 16), share)

    def down_y(q):
        return remote(
            down_hbm.at[0, pl.ds(pl.multiple_of(group * share, 16), share), pl.ds(q * piece, piece)],
            w_down.at[share_rows(block, group), pl.ds(q * piece, piece)],
            wy_s.at[q], wy_r.at[q], other_row,
        )

    def down_x(by, q):
        src = w_down.at[share_rows(far_block, group), pl.ds(q * piece, piece)]
        at = (by - 1) * CHUNKS + q
        return remote(src, src, wx_s.at[at], wx_r.at[at], replica(by))

    def down_l(q):
        src = w_down.at[share_rows(far_block, group), pl.ds(q * piece, piece)]
        return remote(src, src, wl_s.at[q], wl_r.at[q], other_core)

    def down_m(by):
        src = w_down.at[share_rows(far_block, (group + groups - by) % groups)]
        return remote(src, src, wm_s.at[by - 1], wm_r.at[by - 1], other_core)

    down_c = remote(
        down_hbm.at[0], w_down.at[block_rows(block)], wc_s.at[0], wc_r.at[0], other_core
    )

    def relay(q):
        down_y(q).wait_recv()
        for by in range(1, groups):
            down_x(by, q).start()
        down_l(q).start()
        if q + 2 < CHUNKS:
            down_y(q + 2).start()

    down_y(0).start()
    down_y(1).start()
    down_c.start()

    lane = lax.broadcasted_iota(jnp.int32, (tok, LANES), 1)
    named = []
    for k in range(2):
        rel = routes[:, k : k + 1] - z
        rel = jnp.where(rel < 0, rel + experts, rel)
        named.append(rel)
    hits = [(lane == rel).astype(F32) for rel in named]
    lower = (
        lax.broadcasted_iota(jnp.int32, (tok, tok), 0)
        > lax.broadcasted_iota(jnp.int32, (tok, tok), 1)
    ).astype(F32).astype(BF16)
    ranks = jnp.dot(lower, (hits[0] + hits[1]).astype(BF16), preferred_element_type=F32)
    places = lax.broadcasted_iota(jnp.int32, (tok, total), 1).astype(F32)
    chosen = []
    for k in range(2):
        rank = jnp.sum(ranks * hits[k], axis=1, keepdims=True)
        place = named[k].astype(F32) * F32(slot) + rank
        chosen.append((places == place).astype(F32))
    chooser = (chosen[0] + chosen[1]).T.astype(BF16)
    mixing = gates[:, 0:1] * chosen[0] + gates[:, 1:2] * chosen[1]
    mix_hi = mixing.astype(BF16)
    mix_lo = (mixing - mix_hi.astype(F32)).astype(BF16)

    own = pl.multiple_of((row * 2 + core) * slot, 16)
    packed_scale = jnp.dot(chooser, scales[...], preferred_element_type=F32).astype(BF16)
    recv[pl.ds(own, slot), pl.ds(width, LANES)] = packed_scale[:slot]
    pack[:, pl.ds(width, LANES)] = packed_scale[slot:]

    @pl.loop(0, width // tile)
    def _(n):
        cols = pl.ds(pl.multiple_of(n * tile, tile), tile)
        rows = jnp.dot(chooser, decode(codes[:, cols]), preferred_element_type=F32).astype(BF16)
        recv[pl.ds(own, slot), cols] = rows[:slot]
        pack[:, cols] = rows[slot:]

    def packet(step, yy, cc):
        return recv.at[pl.ds(pl.multiple_of(step * quarter + (yy * 2 + cc) * slot, 16), slot)]

    def slab(ref, step):
        return ref.at[pl.ds(pl.multiple_of(step * slot, 16), slot)]

    def send_z(step):
        return remote(
            slab(pack, step - 1), packet(step, row, core), z_s.at[step], z_r.at[step],
            device(ahead(step), row, core),
        )

    def send_y(step):
        src = packet(step, row, core)
        return remote(src, src, y_s.at[step], y_r.at[step], other_row)

    def send_c(step):
        src = packet(step, row, core)
        return remote(src, src, c_s.at[step], c_r.at[step], other_core)

    def send_l(step):
        src = packet(step, 1 - row, core)
        return remote(src, src, l_s.at[step], l_r.at[step], other_core)

    def hid_rows(step, yy, cc):
        return pl.ds(pl.multiple_of(step * quarter + (yy * 2 + cc) * slot, 16), slot)

    def step_rows(step):
        return pl.ds(pl.multiple_of(step * slot, 16), slot)

    own_cols = pl.ds(pl.multiple_of(block * ff, LANES), ff)

    def send_v(step, number):
        yy = 1 - row if number > 0 else row
        cc = 1 - core if number != 1 else core
        return remote(
            hid.at[hid_rows(step, yy, cc)], mine.at[step_rows(step), own_cols],
            v_s.at[step * 3 + number], v_r.at[step * 3 + number], device(z, yy, cc),
        )

    tiles = width // tile
    cuts = (0, (tiles + 1) // 2, tiles)

    def send_h(step, half):
        cols = pl.ds(cuts[half] * tile, (cuts[half + 1] - cuts[half]) * tile)
        return remote(
            hsend.at[step_rows(step), cols], hrecv.at[step_rows(step), cols],
            h_s.at[step * 2 + half], h_r.at[step * 2 + half],
            device(behind(step), row, core),
        )

    def spread(step):
        send_y(step).start()
        send_c(step).start()

    def hidden(step):
        send_y(step).wait_recv()
        send_l(step).start()
        send_c(step).wait_recv()
        send_l(step).wait_recv()
        rows = pl.ds(pl.multiple_of(step * quarter, 16), quarter)

        @pl.loop(0, 2 * ff // 256)
        def _(n):
            cols = pl.ds(pl.multiple_of(n * 256, 256), 256)
            gu[:, cols] = jnp.dot(
                recv[rows, pl.ds(0, width)], w_gu[:, cols], preferred_element_type=F32
            )

        @pl.loop(0, SLICES)
        def _(n):
            some = pl.ds(pl.multiple_of(n * slot, 16), slot)
            where = pl.ds(pl.multiple_of(step * quarter + n * slot, 16), slot)
            scale = recv[where, pl.ds(width, LANES)].astype(F32)[:, :1]
            a = gu[some, pl.ds(0, ff)] * scale
            b = gu[some, pl.ds(ff, ff)] * scale
            hid[where, :] = (a / (1.0 + jnp.exp(-a)) * b).astype(BF16)

        for number in range(3):
            send_v(step, number).start()
        mine[step_rows(step), own_cols] = hid[hid_rows(step, row, core), :]

    def project(step, target, half):
        @pl.loop(cuts[half], cuts[half + 1])
        def _(n):
            cols = pl.ds(pl.multiple_of(n * tile, tile), tile)
            target[step_rows(step), cols] = jnp.dot(
                mine[step_rows(step), :], w_down[:, cols], preferred_element_type=F32
            ).astype(BF16)

    send_z(1).start()
    relay(0)
    relay(1)
    send_z(1).wait_recv()
    spread(1)
    if experts > 2:
        send_z(2).start()
    for q in range(2, CHUNKS):
        relay(q)
    for load in loads:
        load.wait()
    hidden(1)
    for by in range(1, groups):
        for q in range(CHUNKS):
            down_x(by, q).wait_recv()
        down_m(by).start()

    def one_group(step, carry):
        @pl.when(step + 1 < experts)
        def _():
            send_z(step + 1).wait_recv()
            spread(step + 1)

        @pl.when(step + 2 < experts)
        def _():
            send_z(step + 2).start()

        @pl.when(step == 1)
        def _():
            down_c.wait_recv()
            for q in range(CHUNKS):
                down_l(q).wait_recv()
            for by in range(1, groups):
                down_m(by).wait_recv()

        for number in range(3):
            send_v(step, number).wait_recv()
        for half in range(2):
            project(step, hsend, half)
            send_h(step, half).start()

        @pl.when(step == experts - 2)
        def _():
            spread(0)

        @pl.when(step + 1 < experts)
        def _():
            hidden(step + 1)

        return carry

    lax.fori_loop(1, experts, one_group, 0)
    hidden(0)
    for number in range(3):
        send_v(0, number).wait_recv()
    for half in range(2):
        project(0, hrecv, half)

    for step in range(1, experts):
        for half in range(2):
            send_h(step, half).wait_recv()

    @pl.loop(0, width // tile)
    def _(n):
        cols = pl.ds(pl.multiple_of(n * tile, tile), tile)
        rows = hrecv[:, cols]
        out[:, cols] = (
            jnp.dot(mix_hi, rows, preferred_element_type=F32)
            + jnp.dot(mix_lo, rows, preferred_element_type=F32)
        ).astype(BF16)

    for q in range(CHUNKS):
        down_y(q).wait_send()
        down_l(q).wait_send()
        for by in range(1, groups):
            down_x(by, q).wait_send()
    for by in range(1, groups):
        down_m(by).wait_send()
    down_c.wait_send()
    for step in range(experts):
        send_y(step).wait_send()
        send_c(step).wait_send()
        send_l(step).wait_send()
        for number in range(3):
            send_v(step, number).wait_send()
        if step > 0:
            send_z(step).wait_send()
            for half in range(2):
                send_h(step, half).wait_send()


def local(token_codes, scales, routes, route_gates, gate_proj, up_proj, down_proj):
    tok, width = token_codes.shape
    ff = gate_proj.shape[2]
    experts = lax.axis_size("ctx") // SLICES
    cap = 3 * tok * routes.shape[1] // (2 * experts)
    slot = -(-cap // 16) * 16
    total = experts * slot
    vmem = pl.BlockSpec(memory_space=pltpu.VMEM)
    hbm = pl.BlockSpec(memory_space=pl.ANY)
    dma = pltpu.SemaphoreType.DMA
    groups = lax.axis_size("groups")
    far = max(1, (groups - 1) * CHUNKS)
    return pl.pallas_call(
        functools.partial(kernel, experts, slot, 512),
        out_shape=jax.ShapeDtypeStruct((tok, width), BF16),
        in_specs=[vmem] * 4 + [hbm] * 3,
        out_specs=vmem,
        scratch_shapes=[
            pltpu.VMEM((width, 2 * ff), BF16),
            pltpu.VMEM((SLICES * ff, width), BF16),
            pltpu.VMEM((total - slot, width + LANES), BF16),
            pltpu.VMEM((SLICES * total, width + LANES), BF16),
            pltpu.VMEM((SLICES * slot, 2 * ff), F32),
            pltpu.VMEM((SLICES * total, ff), BF16),
            pltpu.VMEM((total, SLICES * ff), BF16),
            pltpu.VMEM((total, width), BF16),
            pltpu.VMEM((total, width), BF16),
            dma((3,)),
            dma((experts,)), dma((experts,)), dma((experts,)), dma((experts,)),
            dma((experts,)), dma((experts,)), dma((experts,)), dma((experts,)),
            dma((3 * experts,)), dma((3 * experts,)),
            dma((2 * experts,)), dma((2 * experts,)),
            dma((CHUNKS,)), dma((CHUNKS,)), dma((far,)), dma((far,)),
            dma((CHUNKS,)), dma((CHUNKS,)), dma((groups,)), dma((groups,)),
            dma((1,)), dma((1,)),
        ],
        compiler_params=pltpu.CompilerParams(
            collective_id=0, has_side_effects=True, vmem_limit_bytes=60 * 2**20
        ),
    )(
        token_codes,
        jnp.broadcast_to(scales[:, None], (tok, LANES)),
        routes,
        route_gates,
        gate_proj,
        up_proj,
        down_proj,
    )


def solution(mesh):
    placed = (
        P(("groups", "ctx"), None),
        P(("groups", "ctx")),
        P(("groups", "ctx"), None),
        P(("groups", "ctx"), None),
        P("ctx", None, None),
        P("ctx", None, None),
        P("ctx", None, None),
    )
    return jax.shard_map(
        local, mesh=mesh, in_specs=placed, out_specs=P(("groups", "ctx"), None), check_vma=False
    )
```
